128 devices in a mesh: pool: 8 (over x, y_hi), tp: 16 (over z, y_lo, core).
Axes of the slice: x: 4, y: 4 (y_hi: 2, y_lo: 2; y = y_hi * 2 + y_lo), z: 4, core: 2. Of those that a mesh axis runs over, the one named last changes fastest.
Arguments:
- tokens: bfloat16 [4096, 8192], P(('pool', 'tp')), may hold values from -6 to 6
- query_weight: bfloat16 [8192, 8192], P(None, 'tp'), may hold values from -0.078125 to 0.078125
- kv_weight: bfloat16 [16, 4096, 256], P('tp'), may hold values from -0.125 to 0.125
- out_weight: bfloat16 [8192, 8192], P('tp'), may hold values from -0.0625 to 0.0625
- prefix_pool: bfloat16 [8, 16, 3, 16, 256, 256], P('pool', None, None, 'tp'), may hold values from -184 to 184, as said below
- block_holder: int32 [16, 12, 1], replicated, may hold values from 0 to 7; in each aligned block of 12 rows (0 to 11, 12 to 23, ..., all dimensions but the last counted through in order) at most 3 rows name the same one
- block_len: int32 [16, 12], replicated, may hold values from 1 to 512, 4608 in all within a row
- mirror_holder: int32 [16], replicated, may hold values from 0 to 7
- group_request: int32 [8], replicated, may hold values from 0 to 15, as said below
Outputs:
- attn_out: bfloat16 [4096, 8192], P(('pool', 'tp'))
- mirror_pool: bfloat16 [8, 8, 512, 2048], P('pool', None, None, 'tp')
The draws below stay inside these ranges and needn't reach their ends.
Inputs may be any that keep to these rules, and one draw needn't show every extreme that they name: `block_holder`: at most 3 of one request's 12 blocks lie on one holder, and some holder has exactly 3 of some request's blocks. `block_len`: the lengths of one request's blocks sum to 4608. `group_request`: the 8 entries are distinct requests. `prefix_pool`: slots that no block uses and tokens past a block's length hold values that no output reads.
All inputs are finite; a program needn't handle non-finite values.
Results may differ from the reference program's by a relative error of at most 0.025.
Values may be sent and summed in bfloat16 or wider, within the bound.
A program may use at most 128 MiB of HBM per device.

```python
import math
import jax
import jax.numpy as jnp
import numpy as np
from jax import lax

D = 8192
HEADS = 64
KVH = 8
HD = 128
NEW = 512
BLK = 512
NB = 12
CAP = 3
PREFIX = 4608
REQS = 16
N_POOL = 8
N_TP = 16


def draw_prefix_pool(key, part):
    key = jax.random.fold_in(key, 11)
    shape = (N_POOL, REQS, CAP, 2 * KVH, BLK // 2, 2 * HD)
    base = 2.0 * jax.random.truncated_normal(key, -6.0, 6.0, shape, jnp.float32)
    return base.astype(jnp.bfloat16)


def draw_group_request(key, part):
    key = jax.random.fold_in(key, 23)
    order = jax.random.permutation(key, REQS).astype(jnp.int32)
    last_place = jnp.argmax((order == REQS - 1).astype(jnp.int32)).astype(jnp.int32)
    target = jax.random.randint(jax.random.fold_in(key, 1), (), 0, N_POOL).astype(jnp.int32)
    moved = order[target]
    order = order.at[last_place].set(moved)
    order = order.at[target].set(REQS - 1)
    return order[:N_POOL].astype(jnp.int32)


def set_ends(values, rng, least, high):
    dims = values.shape
    place = [jax.random.randint(jax.random.fold_in(rng, axis), (), 0, dims[axis]) for axis in range(len(dims))]
    values = values.at[tuple(place)].set(least)
    longest = dims.index(max(dims))
    place[longest] = (place[longest] + 1) % dims[longest]
    return values.at[tuple(place)].set(high)


def block_scale(rng, extent, pieces, low, high):
    def one(axis_at, blocks):
        draws = jax.random.uniform(jax.random.fold_in(jax.random.fold_in(rng, 6), axis_at), (blocks,), jnp.float32, low / len(pieces), high / len(pieces))
        return jnp.repeat(jnp.exp(draws), extent[axis_at] // blocks).reshape((-1,) + (1,) * (len(extent) - axis_at - 1))

    level = one(*pieces[0])
    for cut in pieces[1:]:
        level = level * one(*cut)
    return level


def split_up(number_of, total, limit, lean):
    portions = [(1 << 20) // math.isqrt(grade ** lean) + 1 for grade in range(2, number_of + 1)]
    spare, holding = total - limit - (number_of - 1), [1] * (number_of - 1)
    while spare > 0:
        free = [i for i in range(number_of - 1) if holding[i] < limit]
        pool, left = sum([portions[i] for i in free]), spare
        for i in free:
            more = min(limit - holding[i], max(1, left * portions[i] // pool), spare)
            holding[i] = holding[i] + more
            spare = spare - more
    return np.array([limit] + holding)


def uneven_parts(own_key, amount, total, bound, slope):
    if amount == 2:
        one = jax.random.randint(own_key, (), max(1, total - bound), min(bound, total - 1) + 1)
        return jnp.stack([one, total - one])
    sizes = jnp.asarray(split_up(amount, total, bound, slope), jnp.int32)
    twos = (amount - 1) // 2
    source_of, taker = sizes[1:1 + 2 * twos:2], sizes[2:2 + 2 * twos:2]
    slack = jnp.minimum(source_of - 1, bound - taker)
    passed = jax.random.randint(jax.random.fold_in(own_key, 1), (twos,), 0, 1 << 20) % (slack + 1)
    sizes = sizes.at[1:1 + 2 * twos:2].set(source_of - passed).at[2:2 + 2 * twos:2].set(taker + passed)
    return sizes[jax.random.permutation(jax.random.fold_in(own_key, 2), amount)]


def assign_block(own_key, own, number, rows, amount, top, reach, slope):
    ranking = jax.random.permutation(own_key, amount)
    packed, common = load_shares(amount, rows * top, reach, slope, True), load_shares(amount, rows * top, reach, slope, False)
    places = jnp.arange(amount)

    def named(sizes, rotation):
        used = int((sizes > 0).sum())
        fixed = max(1, used // 4)
        moved = fixed + (places - fixed + rotation * (used - fixed)) % max(1, amount - fixed)
        return jnp.zeros((amount,), jnp.int32).at[ranking[jnp.where(places < fixed, places, moved)]].set(jnp.asarray(sizes, jnp.int32))

    sizes = jnp.where(number % 4 == 0, named(packed, number // 4), named(common, number - number // 4 - 1))
    mixed = jax.random.permutation(jax.random.fold_in(own, 3), amount)
    donor, sink = mixed[0:amount // 2 * 2:2], mixed[1:amount // 2 * 2:2]
    margin = jnp.minimum(sizes[donor] - 1, reach - sizes[sink]) // 2
    margin = jnp.where((donor == ranking[0]) | (sink == ranking[0]) | (sizes[sink] == 0), 0, jnp.maximum(margin, 0))
    moved = jax.random.randint(jax.random.fold_in(own, 4), (amount // 2,), 0, 1 << 20) % (margin + 1)
    sizes = sizes.at[donor].add(-moved).at[sink].add(moved)
    labels = jnp.searchsorted(jnp.cumsum(sizes), jnp.arange(rows * top), side="right").astype(jnp.int32)
    grid = labels.reshape(top, rows).T
    grid = grid[jax.random.permutation(jax.random.fold_in(own, 1), rows)]
    rotation = jax.random.randint(jax.random.fold_in(own, 2), (rows, 1), 0, top)
    return jnp.take_along_axis(grid, (jnp.arange(top)[None, :] + rotation) % top, axis=1)


def load_shares(number_of, total, reach, slope, full):
    weights = [(1 << 20) // math.isqrt(standing ** slope) + 1 for standing in range(1, number_of + 1)]
    largest = reach if full else min(reach, max(-(-total // number_of), total * weights[0] // sum(weights)))
    least = 1 if total - largest >= number_of - 1 else 0
    given, surplus = [largest] + [least] * (number_of - 1), total - largest - least * (number_of - 1)
    while surplus > 0:
        free = [i for i in range(1, number_of) if given[i] < largest] or [i for i in range(1, number_of) if given[i] < reach]
        pool, budget = sum([weights[i] for i in free]), surplus
        for i in free:
            more = min(reach - given[i], max(1, budget * weights[i] // pool), surplus)
            given[i] = given[i] + more
            surplus = surplus - more
    return np.array(given)


def normal_values(own_key, dims, spread, limit, pieces=(), held_as=jnp.bfloat16):
    values = spread * jax.random.normal(own_key, dims, jnp.float32)
    if pieces:
        values = values * block_scale(own_key, dims, pieces, -0.22, 0.18)
    return jnp.clip(values, -limit, limit).astype(held_as)


def setup_inputs(seed: int = 0) -> dict:
    keys = jax.random.split(jax.random.key(seed), 10)
    tokens = normal_values(keys[0], (N_POOL * NEW, D), 1.0, 6.0, ((0, 128),))
    query_weight = normal_values(keys[1], (D, HEADS * HD), (D * 16 // 25) ** -0.5, 0.078125, ((1, 16),))
    kv_weight = normal_values(keys[2], (2 * KVH, D // 2, 2 * HD), (D // 4) ** -0.5, 0.125, ((0, 16),))
    out_weight = normal_values(keys[3], (HEADS * HD, D), (HEADS * HD) ** -0.5, 0.0625, ((0, 16),))
    prefix_pool = draw_prefix_pool(jax.random.fold_in(keys[9], 71), 0)
    block_holder_keys = jax.random.split(jax.random.fold_in(keys[5], 1), REQS * NB // NB)
    block_holder_turns = jax.random.permutation(jax.random.fold_in(keys[5], 3), REQS * NB // NB)
    block_holder = jax.vmap(lambda own, number: assign_block(jax.random.fold_in(keys[5], 2), own, number, NB, N_POOL, 1, CAP, 2))(block_holder_keys, block_holder_turns).reshape((REQS, NB, 1))
    block_len = jax.vmap(lambda own: uneven_parts(own, NB, PREFIX, BLK, 2))(jax.random.split(keys[6], REQS)).reshape((REQS, NB)).astype(jnp.int32)
    mirror_holder = set_ends(jax.random.randint(keys[7], (REQS,), 0, N_POOL), jax.random.fold_in(keys[7], 1), 0, N_POOL - 1).astype(jnp.int32)
    group_request = draw_group_request(jax.random.fold_in(keys[9], 71), 0)
    return dict(tokens=tokens, query_weight=query_weight, kv_weight=kv_weight, out_weight=out_weight, prefix_pool=prefix_pool, block_holder=block_holder, block_len=block_len, mirror_holder=mirror_holder, group_request=group_request)


ROPE_BASE = 500000.0
NORM_EPS = 1e-05
MASKED = -1e+30

def rotate(values, positions):
    halfway = values.shape[-1] // 2
    frequency = ROPE_BASE ** (-(jnp.arange(halfway).astype(jnp.float32) * 2.0 / values.shape[-1]))
    angles = positions[:, None] * frequency[None, :]
    cosine = jnp.cos(angles)[:, None, :]
    sine_part = jnp.sin(angles)[:, None, :]
    first_half = values[..., :halfway]
    second_half = values[..., halfway:]
    return jnp.concatenate([first_half * cosine - second_half * sine_part, second_half * cosine + first_half * sine_part], axis=-1)

def slot_ranks(holders, holder_count):
    onehot = (holders[:, None] == jnp.arange(holder_count, dtype=jnp.int32)[None, :]).astype(jnp.int32)
    before = jnp.cumsum(onehot, axis=0) - onehot
    return lax.optimization_barrier(jnp.sum(onehot * before, axis=1)).astype(jnp.int32)

def reference(tokens, query_weight, kv_weight, out_weight, prefix_pool, block_holder, block_len, mirror_holder, group_request):
    groups = N_POOL
    query_rows = NEW
    activations = tokens.astype(jnp.float32)
    normed = (activations * lax.rsqrt(lax.optimization_barrier(jnp.mean(activations * activations, axis=-1, keepdims=True)) + NORM_EPS)).astype(jnp.bfloat16)
    full_kv = kv_weight.reshape(KVH, 2, D // 2, 2 * HD).transpose(1, 2, 0, 3).reshape(D, KVH * 2 * HD)
    queries = jnp.dot(normed, query_weight, preferred_element_type=jnp.float32).reshape(groups * query_rows, HEADS, HD)
    pairs = jnp.dot(normed, full_kv, preferred_element_type=jnp.float32).reshape(groups * query_rows, KVH, 2, HD)
    positions = (jnp.arange(groups * query_rows) % query_rows).astype(jnp.float32) + PREFIX
    queries = rotate(queries, positions).astype(jnp.bfloat16)
    keys_new = rotate(pairs[:, :, 0], positions).astype(jnp.bfloat16)
    values_new = pairs[:, :, 1].astype(jnp.bfloat16)
    fresh_pairs = jnp.stack([keys_new, values_new], axis=2).reshape(groups, query_rows, KVH * 2 * HD)
    holder_ids = jnp.arange(groups, dtype=jnp.int32)
    group_mirror = jnp.take(mirror_holder, group_request, axis=0)
    select = group_mirror[None, :] == holder_ids[:, None]
    mirror_pool = jnp.where(select[:, :, None, None], fresh_pairs[None], jnp.zeros((), jnp.bfloat16)).astype(jnp.bfloat16)
    causal = jnp.arange(query_rows)[:, None] >= jnp.arange(query_rows)[None, :]

    def attend_group(group):
        request = group_request[group]
        holders = block_holder[request, :, 0]
        lengths = block_len[request]
        ranks = slot_ranks(holders, groups)
        picked = prefix_pool[holders, request, ranks]
        blocks = picked.reshape(NB, KVH, 2, BLK // 2, 2, HD).transpose(0, 2, 3, 1, 4, 5).reshape(NB * BLK, KVH, 2, HD)
        live = (jnp.arange(BLK)[None, :] < lengths[:, None]).reshape(NB * BLK)
        first_row = (group * query_rows).astype(jnp.int32)
        own_queries = lax.dynamic_slice_in_dim(queries, first_row, query_rows, 0)
        own_keys = lax.dynamic_slice_in_dim(keys_new, first_row, query_rows, 0)
        own_values = lax.dynamic_slice_in_dim(values_new, first_row, query_rows, 0)
        all_keys = jnp.concatenate([blocks[:, :, 0], own_keys], axis=0).transpose(1, 0, 2)
        all_values = jnp.concatenate([blocks[:, :, 1], own_values], axis=0).transpose(1, 0, 2)
        allowed = jnp.concatenate([jnp.broadcast_to(live[None, :], (query_rows, NB * BLK)), causal], axis=1)
        grouped = own_queries.reshape(query_rows, KVH, HEADS // KVH, HD).transpose(1, 2, 0, 3)

        def one_head(head_items):
            head_queries, head_keys, head_values = head_items
            scores = jnp.einsum('qcd,kd->qck', head_queries.astype(jnp.float32), head_keys.astype(jnp.float32)) / math.sqrt(HD)
            scores = jnp.where(allowed[None], scores, MASKED)
            largest = lax.optimization_barrier(jnp.max(scores, axis=-1, keepdims=True))
            weights = jnp.exp(scores - largest)
            total = lax.optimization_barrier(jnp.sum(weights, axis=-1, keepdims=True))
            rounded = lax.optimization_barrier(weights.astype(jnp.bfloat16))
            summed = jnp.einsum('qck,kd->qcd', rounded.astype(jnp.float32), head_values.astype(jnp.float32))
            return summed / total
        outputs = lax.map(one_head, (grouped, all_keys, all_values))
        return outputs.transpose(2, 0, 1, 3).reshape(query_rows, HEADS * HD).astype(jnp.bfloat16)
    attended = lax.map(attend_group, jnp.arange(groups, dtype=jnp.int32)).reshape(groups * query_rows, HEADS * HD)
    share_width = HEADS * HD // N_TP

    def add_share(share_index, running):
        first_col = (share_index * share_width).astype(jnp.int32)
        columns = lax.dynamic_slice_in_dim(attended, first_col, share_width, 1)
        weight_rows = lax.dynamic_slice_in_dim(out_weight, first_col, share_width, 0)
        partial_value = jnp.dot(columns, weight_rows, preferred_element_type=jnp.float32).astype(jnp.bfloat16)
        return running + lax.optimization_barrier(partial_value).astype(jnp.float32)
    summed_out = lax.fori_loop(0, N_TP, add_share, jnp.zeros((groups * query_rows, D), jnp.float32))
    return (summed_out.astype(jnp.bfloat16), mirror_pool)
```

```python
import functools
import math

import jax
import jax.numpy as jnp
from jax import lax
from jax.experimental import pallas as pl
from jax.experimental.pallas import tpu as pltpu
from jax.sharding import PartitionSpec as P

KVH = 8
HD = 128
PREFIX = 4608
NEW = 512
NB = 12
ROPE_BASE = 500000.0
NORM_EPS = 1e-05
LOG2E = 1.4426950408889634
DEAD = -(2.0**93)
TILE = 16
TILES = 304
PRE = TILES * TILE
KEY_CHUNKS = (512,) * 9 + (768,)
MESH = pl.DeviceIdType.MESH


def swapped(block, axis, bit):
    count = lax.axis_size(axis)
    route = []
    for low in range(count):
        high = low | 1 << bit
        if high != low and high < count:
            route += [(low, high), (high, low)]
    return lax.ppermute(block, axis, route)


def rotate(values, positions):
    halfway = values.shape[-1] // 2
    frequency = ROPE_BASE ** (-(jnp.arange(halfway).astype(jnp.float32) * 2.0 / values.shape[-1]))
    angles = positions[:, None] * frequency[None, :]
    cosine = jnp.cos(angles)[:, None, :]
    sine_part = jnp.sin(angles)[:, None, :]
    first_half = values[..., :halfway]
    second_half = values[..., halfway:]
    return jnp.concatenate(
        [
            first_half * cosine - second_half * sine_part,
            second_half * cosine + first_half * sine_part,
        ],
        axis=-1,
    )


def tile_lists(lengths, slots, slot_tiles):
    tiles = (lengths + TILE - 1) // TILE
    ends = jnp.cumsum(tiles)
    place = jnp.arange(TILES, dtype=jnp.int32)
    block = jnp.sum((place[:, None] >= ends[None, :]).astype(jnp.int32), axis=1)
    onehot = (block[:, None] == jnp.arange(NB, dtype=jnp.int32)[None, :]).astype(jnp.int32)
    within = place - jnp.sum(onehot * (ends - tiles)[None, :], axis=1)
    slot = jnp.sum(onehot * slots[None, :], axis=1)
    length = jnp.sum(onehot * lengths[None, :], axis=1)
    live = jnp.clip(length - within * TILE, 0, TILE)
    source = jnp.where(block < NB, slot * slot_tiles + within, 0)
    return source.astype(jnp.int32), live.astype(jnp.int32)


def pack_prefix(source, live, kv, fresh, keys, values):
    row = lax.broadcasted_iota(jnp.int32, (TILE, HD), 0)

    def one(n, carry):
        start = pl.multiple_of(source[n] * TILE, TILE)
        to = pl.ds(pl.multiple_of(n * TILE, TILE), TILE)
        keys[to, 0:HD] = kv[pl.ds(start, TILE), 0:HD]
        values[to, 0:HD] = kv[pl.ds(start, TILE), HD : 2 * HD]
        keys[to, HD : 2 * HD] = jnp.where(row < live[n], 0.0, DEAD).astype(jnp.bfloat16)
        return carry

    lax.fori_loop(0, TILES, one, 0, unroll=8)
    keys[PRE:, 0:HD] = fresh[:, 0:HD]
    keys[PRE:, HD : 2 * HD] = jnp.zeros((NEW, HD), jnp.bfloat16)
    values[PRE:, 0:HD] = fresh[:, HD : 2 * HD]
    values[:, HD : 2 * HD] = jnp.ones((PRE + NEW, HD), jnp.bfloat16)


def attend_rows(queries, keys, values, first_row, rows):
    count = queries.shape[0]
    queries = jnp.concatenate([queries, jnp.ones((count, HD), jnp.bfloat16)], axis=1)
    top, total, start = None, None, 0
    for size in KEY_CHUNKS:
        stop = start + size
        scores = lax.dot_general(
            queries,
            keys[start:stop, :],
            (((1,), (1,)), ((), ())),
            preferred_element_type=jnp.float32,
        )
        if stop > PRE:
            lead = size - NEW
            key = lax.broadcasted_iota(jnp.int32, (rows, NEW), 1)
            place = lax.broadcasted_iota(jnp.int32, (rows, NEW), 0) + first_row
            seen = jnp.concatenate([key <= place] * (count // rows), axis=0)
            tail = jnp.where(seen, scores[:, lead:], DEAD)
            scores = jnp.concatenate([scores[:, :lead], tail], axis=1)
        largest = jnp.max(scores, axis=1, keepdims=True)
        if top is not None:
            largest = jnp.maximum(top, largest)
        weights = jnp.exp2(scores - largest).astype(jnp.bfloat16)
        part = jnp.dot(weights, values[start:stop, :], preferred_element_type=jnp.float32)
        total = part if top is None else total * jnp.exp2(top - largest) + part
        top, start = largest, stop
    return total[:, :HD] / total[:, HD:]


def attend_kernel(source, live, queries, fresh, kv, out, keys, values):
    pack_prefix(source, live, kv, fresh, keys, values)
    rows, heads = 128, queries.shape[1] // HD

    def one(step, carry):
        first = pl.multiple_of(step * rows, rows)
        here = pl.ds(first, rows)
        stacked = jnp.concatenate(
            [queries[here, h * HD : (h + 1) * HD] for h in range(heads)], axis=0
        )
        done = attend_rows(stacked, keys, values, first, rows).astype(jnp.bfloat16)
        for h in range(heads):
            out[here, h * HD : (h + 1) * HD] = done[h * rows : (h + 1) * rows]
        return carry

    lax.fori_loop(0, NEW // rows, one, 0)


def attend(source, live, queries, fresh, kv):
    return pl.pallas_call(
        attend_kernel,
        out_shape=jax.ShapeDtypeStruct(queries.shape, jnp.bfloat16),
        in_specs=[pl.BlockSpec(memory_space=pltpu.SMEM)] * 2
        + [pl.BlockSpec(memory_space=pltpu.VMEM)] * 3,
        out_specs=pl.BlockSpec(memory_space=pltpu.VMEM),
        scratch_shapes=[pltpu.VMEM((PRE + NEW, 2 * HD), jnp.bfloat16)] * 2,
        compiler_params=pltpu.CompilerParams(vmem_limit_bytes=56 << 20),
        cost_estimate=pl.CostEstimate(
            flops=10_000_000_000, bytes_accessed=8 << 20, transcendentals=11_000_000
        ),
    )(source, live, queries, fresh, kv)


def places():
    pool, tp = lax.axis_index("pool"), lax.axis_index("tp")
    z, y, core = tp // 4, (tp // 2) % 2, tp % 2
    up = (pool, ((z + 1) % 4) * 4 + y * 2 + core)
    down = (pool, ((z + 3) % 4) * 4 + y * 2 + core)
    across = (pool, z * 4 + (1 - y) * 2 + core)
    twin = (pool, z * 4 + y * 2 + 1 - core)
    return z, y, core, up, down, across, twin


def greet(partners):
    barrier = pltpu.get_barrier_semaphore()
    for partner in partners:
        pl.semaphore_signal(barrier, inc=1, device_id=partner, device_id_type=MESH)
    pl.semaphore_wait(barrier, len(partners))


PARTS = ("y", "z", "y", "z")
WIDE = 1024
HALF = WIDE // 2


def out_kernel(attended, weight, twin_weight, out, mine, other, w_mine, w_other, *scratch):
    parts, scratch = scratch[:4], scratch[4:]
    from_y, low_first, high_first, low_last, high_last, kept = (
        scratch[0:4],
        scratch[4:8],
        scratch[8:12],
        scratch[12:16],
        scratch[16:20],
        scratch[20:24],
    )
    to_y, to_twin, from_twin, sent, got, loads = scratch[24:30]
    z, y, core, up, down, across, twin = places()
    loading = []
    for p in range(4):
        column = pl.multiple_of(core * (4 * WIDE) + p * WIDE, WIDE)
        loading.append(
            (
                pltpu.make_async_copy(
                    weight.at[:, pl.ds(column, WIDE)], w_mine.at[p], loads.at[2 * p]
                ),
                pltpu.make_async_copy(
                    twin_weight.at[:, pl.ds(p * WIDE, WIDE)], w_other.at[p], loads.at[2 * p + 1]
                ),
            )
        )
        for copy in loading[p]:
            copy.start()
    for k in range(4):
        first = pl.multiple_of(((z + k) % 4) * 128, 128)
        mine[k * 128 : (k + 1) * 128, :] = attended[pl.ds(first, 128), :]
    greet((up, down, across, twin))
    counter = [0]
    copies = []

    def send(source, target, device):
        n = counter[0]
        counter[0] += 1
        copy = pltpu.make_async_remote_copy(
            src_ref=source,
            dst_ref=target,
            send_sem=sent.at[n],
            recv_sem=got.at[n],
            device_id=device,
            device_id_type=MESH,
        )
        copy.start()
        copies.append(copy)
        return copy

    exchange = send(mine, other, twin)
    exchange.wait_recv()
    arriving = {}
    own_y = pl.ds(pl.multiple_of(y * 64, 64), 64)
    their_y = pl.ds(pl.multiple_of((1 - y) * 64, 64), 64)

    def multiply(p):
        for copy in loading[p]:
            copy.wait()
        total = jnp.dot(mine[...], w_mine[p], preferred_element_type=jnp.float32)
        total = total + jnp.dot(other[...], w_other[p], preferred_element_type=jnp.float32)
        parts[p][...] = total.astype(jnp.bfloat16).reshape(4, 128, WIDE)

    def rows_of(p):
        return own_y if PARTS[p] == "y" else pl.ds(0, 128)

    def start_y(p):
        arriving["y", p] = send(parts[p].at[:, their_y, :], from_y[p], across)

    def take_y(p):
        arriving["y", p].wait_recv()
        for k in range(4):
            total = parts[p][k, own_y, :].astype(jnp.float32) + from_y[p][k].astype(jnp.float32)
            parts[p][k, own_y, :] = total.astype(jnp.bfloat16)

    def start_z(p):
        rows = rows_of(p)
        low, high = pl.ds(0, HALF), pl.ds(HALF, HALF)
        arriving["a+", p] = send(parts[p].at[2, rows, low], low_first[p], up)
        arriving["a-", p] = send(parts[p].at[2, rows, high], high_first[p], down)
        arriving["b+", p] = [send(parts[p].at[1, rows, high], low_last[p].at[:, high], up)]
        arriving["b-", p] = [send(parts[p].at[3, rows, low], high_last[p].at[:, low], down)]

    def pass_z(p):
        rows = rows_of(p)
        low, high = pl.ds(0, HALF), pl.ds(HALF, HALF)
        arriving["a+", p].wait_recv()
        total = parts[p][1, rows, low].astype(jnp.float32) + low_first[p][...].astype(jnp.float32)
        parts[p][1, rows, low] = total.astype(jnp.bfloat16)
        arriving["b+", p].append(send(parts[p].at[1, rows, low], low_last[p].at[:, low], up))
        arriving["a-", p].wait_recv()
        total = parts[p][3, rows, high].astype(jnp.float32) + high_first[p][...].astype(jnp.float32)
        parts[p][3, rows, high] = total.astype(jnp.bfloat16)
        arriving["b-", p].append(send(parts[p].at[3, rows, high], high_last[p].at[:, high], down))

    def take_z(p):
        for copy in arriving["b+", p] + arriving["b-", p]:
            copy.wait_recv()

    def z_rows(p, rows):
        at = rows if PARTS[p] == "z" else pl.ds(0, 64)
        return (
            parts[p][0, rows, :].astype(jnp.float32)
            + low_last[p][at, :].astype(jnp.float32)
            + high_last[p][at, :].astype(jnp.float32)
        )

    def turn_y(p):
        take_z(p)
        to_y[p] = z_rows(p, their_y).astype(jnp.bfloat16)
        arriving["y", p] = send(to_y.at[p], from_y[p], across)
        kept[p][...] = z_rows(p, own_y)

    def finish(p):
        if PARTS[p] == "z":
            arriving["y", p].wait_recv()
            kept[p][...] += from_y[p][...].astype(jnp.float32)
        else:
            take_z(p)
            kept[p][...] = z_rows(p, own_y)
        my_rows = pl.ds(pl.multiple_of(core * 32, 32), 32)
        twin_rows = pl.ds(pl.multiple_of((1 - core) * 32, 32), 32)
        to_twin[p] = kept[p][twin_rows, :].astype(jnp.bfloat16)
        arriving["c", p] = send(to_twin.at[p], from_twin.at[p], twin)
        column = pl.multiple_of(core * (4 * WIDE) + p * WIDE, WIDE)
        out[:, pl.ds(column, WIDE)] = kept[p][my_rows, :].astype(jnp.bfloat16)

    multiply(0)
    start_y(0)
    multiply(1)
    start_z(1)
    multiply(2)
    start_y(2)
    multiply(3)
    start_z(3)
    pass_z(1)
    pass_z(3)
    take_y(0)
    start_z(0)
    turn_y(1)
    turn_y(3)
    pass_z(0)
    take_y(2)
    start_z(2)
    finish(1)
    finish(0)
    pass_z(2)
    finish(3)
    finish(2)
    for p in (1, 0, 3, 2):
        arriving["c", p].wait_recv()
        column = pl.multiple_of((1 - core) * (4 * WIDE) + p * WIDE, WIDE)
        out[:, pl.ds(column, WIDE)] = from_twin[p]
    for copy in copies:
        copy.wait_send()


def project_out(attended, weight, twin_weight):
    bf16, f32, vmem = jnp.bfloat16, jnp.float32, pltpu.VMEM
    z_rows = [64 if kind == "y" else 128 for kind in PARTS]
    scratch = [vmem((NEW, 512), bf16)] * 2 + [vmem((4, 512, WIDE), bf16)] * 2
    scratch += [vmem((4, 128, WIDE), bf16)] * 4
    scratch += [vmem((4, 64, WIDE) if kind == "y" else (64, WIDE), bf16) for kind in PARTS]
    scratch += [vmem((rows, HALF), bf16) for rows in z_rows] * 2
    scratch += [vmem((rows, WIDE), bf16) for rows in z_rows] * 2
    scratch += [vmem((64, WIDE), f32)] * 4
    scratch += [vmem((4, 64, WIDE), bf16), vmem((4, 32, WIDE), bf16), vmem((4, 32, WIDE), bf16)]
    scratch += [pltpu.SemaphoreType.DMA((33,))] * 2 + [pltpu.SemaphoreType.DMA((8,))]
    return pl.pallas_call(
        out_kernel,
        out_shape=jax.ShapeDtypeStruct((32, 8 * WIDE), bf16),
        in_specs=[
            pl.BlockSpec(memory_space=vmem),
            pl.BlockSpec(memory_space=pl.ANY),
            pl.BlockSpec(memory_space=pl.ANY),
        ],
        out_specs=pl.BlockSpec(memory_space=vmem),
        scratch_shapes=scratch,
        compiler_params=pltpu.CompilerParams(
            collective_id=1, has_side_effects=True, vmem_limit_bytes=56 << 20
        ),
        cost_estimate=pl.CostEstimate(
            flops=4_300_000_000, bytes_accessed=12 << 20, transcendentals=0
        ),
    )(attended, weight, twin_weight)


def local(
    tokens,
    query_weight,
    kv_weight,
    out_weight,
    prefix_pool,
    block_holder,
    block_len,
    mirror_holder,
    group_request,
):
    pool_count = lax.axis_size("pool")
    tp_count = lax.axis_size("tp")
    pool_place = lax.axis_index("pool")
    tp_place = lax.axis_index("tp")
    query_cols = query_weight.shape[1]
    head_count = query_cols // HD
    local_pairs = kv_weight.shape[0]
    half_width = kv_weight.shape[1]
    pair_width = kv_weight.shape[2]
    first_pair = tp_place * local_pairs
    my_half = tp_place % 2
    activations = tokens.astype(jnp.float32)
    normed = (
        activations
        * lax.rsqrt(jnp.mean(activations * activations, axis=-1, keepdims=True) + NORM_EPS)
    ).astype(jnp.bfloat16)
    row_piece = lax.all_gather(normed, "tp", axis=0, tiled=True)
    query_part = jnp.dot(row_piece, query_weight, preferred_element_type=jnp.float32)
    feature_half = (first_pair + 0) % 2
    columns = lax.dynamic_slice_in_dim(row_piece, feature_half * half_width, half_width, 1)
    kv_part = jnp.dot(columns, kv_weight[0], preferred_element_type=jnp.float32)
    projected = jnp.concatenate([query_part, kv_part], axis=1)
    query_rows = projected.shape[0]
    kv_sums = projected[:, query_cols:]
    kv_sums = kv_sums + swapped(kv_sums.astype(jnp.bfloat16), "tp", 0).astype(kv_sums.dtype)
    positions = jnp.arange(query_rows).astype(jnp.float32) + PREFIX
    queries = rotate(
        projected[:, :query_cols].reshape(query_rows, head_count, HD), positions
    )
    queries = (queries * (LOG2E / math.sqrt(HD))).astype(jnp.bfloat16).reshape(query_rows, -1)
    rotated_keys = rotate(kv_sums[:, :HD].reshape(query_rows, 1, HD), positions).reshape(
        query_rows, HD
    )
    fresh_pairs = jnp.concatenate([rotated_keys, kv_sums[:, HD:]], axis=1).astype(jnp.bfloat16)
    mirror_width = 2 * KVH * HD // tp_count
    mirror_start = tp_place * mirror_width % pair_width
    mirror_share = lax.dynamic_slice_in_dim(fresh_pairs, mirror_start, mirror_width, 1)
    everyone = lax.all_gather(mirror_share, "pool", axis=0, tiled=True).reshape(
        pool_count, query_rows, mirror_width
    )
    group_mirror = jnp.take(mirror_holder, group_request, axis=0)
    keep_group = group_mirror == pool_place
    mirror_pool = jnp.where(keep_group[:, None, None], everyone, jnp.zeros((), jnp.bfloat16))[None]
    holder_ids = jnp.arange(pool_count, dtype=jnp.int32)
    request = group_request[pool_place]
    holders = jnp.take(block_holder[:, :, 0], request, axis=0)
    lengths = jnp.take(block_len, request, axis=0)
    onehot = (holders[:, None] == holder_ids[None, :]).astype(jnp.int32)
    before = jnp.cumsum(onehot, axis=0) - onehot
    block_ranks = jnp.sum(onehot * before, axis=1)
    holder_slab = prefix_pool[0]
    slot_count = holder_slab.shape[1]
    fetched = lax.all_to_all(
        jnp.take(holder_slab, group_request, axis=0),
        "pool",
        split_axis=0,
        concat_axis=0,
        tiled=True,
    )
    chosen = fetched.reshape(pool_count * slot_count, -1, pair_width)
    partner_blocks = swapped(chosen, "tp", 0)
    chosen = jnp.where(
        my_half == 0,
        jnp.concatenate([chosen, partner_blocks], axis=1),
        jnp.concatenate([partner_blocks, chosen], axis=1),
    )
    block_tokens = chosen.shape[1]
    source, live = tile_lists(lengths, holders * slot_count + block_ranks, block_tokens // TILE)
    attended = attend(source, live, queries, fresh_pairs, chosen.reshape(-1, pair_width))
    half_cols = out_weight.shape[1] // 2
    twin_weight = swapped(
        lax.dynamic_slice_in_dim(out_weight, (1 - my_half) * half_cols, half_cols, 1), "tp", 0
    )
    attn_out = project_out(attended, out_weight, twin_weight)
    return (attn_out, mirror_pool)


def solution(mesh):
    in_specs = (
        P(("pool", "tp"), None),
        P(None, "tp"),
        P("tp", None, None),
        P("tp", None),
        P("pool", None, None, "tp", None, None),
        P(),
        P(),
        P(),
        P(),
    )
    out_specs = (P(("pool", "tp"), None), P("pool", None, None, "tp"))
    return jax.shard_map(local, mesh=mesh, in_specs=in_specs, out_specs=out_specs, check_vma=False)
```
